32 devices in a mesh: group: 2 (over x), rep: 16 (over z, y, core).
Axes of the slice: x: 2, y: 2, z: 4, core: 2. Of those that a mesh axis runs over, the one named last changes fastest.
Arguments:
- archive: bfloat16 [1024, 32768], P('group', 'rep'), parts along dimension 0, may hold values from -6 to 6
- w_first: bfloat16 [65536, 1024], P(('group', 'rep')), parts along dimension 0, may hold values from -0.03125 to 0.03125
- b_first: float32 [2048], P('group'), parts along dimension 0, may hold values from -1 to 1
- w_second: bfloat16 [2048, 256], P('group'), parts along dimension 0, may hold values from -0.1875 to 0.1875
- pair_table: int32 [4096, 3], P(('group', 'rep')), parts along dimension 0, may hold values from 0 to 127, as said below
Outputs:
- score: float32 [2], P('group'), parts along dimension 0
- grad_first: float32 [65536, 1024], P(('group', 'rep')), parts along dimension 0
- grad_bias: float32 [2048], P('group'), parts along dimension 0
- grad_second: float32 [2048, 256], P('group'), parts along dimension 0
The draws below stay inside these ranges and needn't reach their ends.
There are 2 independent parts, one for each index of `group`. The reference program is written for one: setup_inputs(seed, part) draws one part's arguments, and reference() takes and returns one part's arrays. A program takes and returns all parts, laid end to end along the dimension named above; each array names one. Nothing has to cross between parts.
Inputs may be any that keep to these rules, and one draw needn't show every extreme that they name: `pair_table`: column 1 equals column 0 plus 16; column 2 is a trajectory below 4; columns 0 and 1 are steps within that trajectory.
All inputs are finite; a program needn't handle non-finite values.
Results may differ from the reference program's by a relative error of at most 0.028.
The reference program's roundings to bfloat16 on the way (of `hidden`, `features`, `frame_grad` and `d_pre`) count: a program that leaves them out, or rounds other values in their place, can miss the bound.
Values may be sent and summed in bfloat16 or wider, within the bound.
A program may use at most 128 MiB of HBM per device.

```python
import jax
import jax.numpy as jnp
from jax import lax

FIELD = 32768
HIDDEN_SIZE = 1024
FEAT = 256
TRAJS = 4
FRAMES = 512
PAIRS = 2048
STEPS = 128
TAU = 16


def draw_pair_table(key, part):
    key_begin, key_traj = jax.random.split(jax.random.fold_in(key, 7))
    begin_step = jax.random.randint(key_begin, (PAIRS,), 0, STEPS - TAU)
    trajectory = jax.random.randint(key_traj, (PAIRS,), 0, TRAJS)
    begin_step = begin_step.at[0].set(STEPS - TAU - 1).at[1].set(0)
    return jnp.stack([begin_step, begin_step + TAU, trajectory], axis=1).astype(jnp.int32)


def strengthened(drawn, key, source, target, shards_of, factor):
    def block_of(dim):
        return (jnp.arange(drawn.shape[dim]) // (drawn.shape[dim] // shards_of)).reshape((-1,) + (1,) * (drawn.ndim - 1 - dim))

    one_side = jax.random.permutation(key, shards_of)[block_of(target)]
    other_side = (block_of(target) + shards_of // 2) % shards_of
    return jnp.where((block_of(source) == one_side) | (block_of(source) == other_side), factor * drawn, drawn)


def level_of(rng, extent, cuts, low, high):
    def one(axis_at, parts):
        draws = jax.random.uniform(jax.random.fold_in(jax.random.fold_in(rng, 6), axis_at), (parts,), jnp.float32, low / len(cuts), high / len(cuts))
        return jnp.repeat(jnp.exp(draws), extent[axis_at] // parts).reshape((-1,) + (1,) * (len(extent) - axis_at - 1))

    factor_of = one(*cuts[0])
    for cut in cuts[1:]:
        factor_of = factor_of * one(*cut)
    return factor_of


def centred(own_key, dims, deviation, most, cuts=(), kind=jnp.bfloat16):
    values = deviation * jax.random.normal(own_key, dims, jnp.float32)
    if cuts:
        values = values * level_of(own_key, dims, cuts, -0.22, 0.18)
    return jnp.clip(values, -most, most).astype(kind)


def gaussian_with(rng, dims, scale, most, cuts, heavy, held_as=jnp.bfloat16):
    result = scale * jax.random.normal(rng, dims, jnp.float32)
    if cuts:
        result = result * level_of(rng, dims, cuts, -0.22, 0.18)
    return jnp.clip(strengthened(result, jax.random.fold_in(rng, 3), *heavy), -most, most).astype(held_as)


def setup_inputs(seed: int = 0, part: int = 0) -> dict:
    keys = jax.random.split(jax.random.key(seed), 6)
    part_keys = jax.random.split(jax.random.fold_in(keys[5], part), 6)
    return {
        "archive": gaussian_with(part_keys[0], (FRAMES, FIELD), 1.0, 6.0, ((1, 16),), (1, 0, 16, 2.0)),
        "w_first": centred(part_keys[1], (FIELD, HIDDEN_SIZE), FIELD ** -0.5, 0.03125, ((0, 16),)),
        "b_first": jnp.clip(jax.random.uniform(part_keys[2], (HIDDEN_SIZE,), jnp.float32, -1.0, 1.0), -1.0, 1.0),
        "w_second": centred(part_keys[3], (HIDDEN_SIZE, FEAT), HIDDEN_SIZE ** -0.5, 0.1875),
        "pair_table": draw_pair_table(jax.random.fold_in(jax.random.fold_in(keys[5], part), 71), part),
    }


EPS = 0.001
PRECISE = lax.Precision.HIGHEST

def vamp_score(sum_inst, sum_lag, cov_inst, cov_cross, cov_lag, total_pairs):
    mean_inst = sum_inst / total_pairs
    mean_lag = sum_lag / total_pairs
    identity = jnp.eye(sum_inst.shape[0], dtype=jnp.float32)
    c_inst = cov_inst / total_pairs - mean_inst[:, None] * mean_inst[None, :] + EPS * identity
    c_cross = cov_cross / total_pairs - mean_inst[:, None] * mean_lag[None, :]
    c_lag = cov_lag / total_pairs - mean_lag[:, None] * mean_lag[None, :] + EPS * identity
    chol_inst = jnp.linalg.cholesky(c_inst)
    chol_lag = jnp.linalg.cholesky(c_lag)
    whitened = jax.scipy.linalg.solve_triangular(chol_inst, c_cross, lower=True)
    koopman = jax.scipy.linalg.solve_triangular(chol_lag, whitened.T, lower=True)
    return 1.0 + jnp.sum(koopman * koopman)

def score_grads(stats, total_pairs):

    def wrapped(sum_inst, sum_lag, cov_inst, cov_cross, cov_lag):
        return vamp_score(sum_inst, sum_lag, cov_inst, cov_cross, cov_lag, total_pairs)
    value, pullback = jax.vjp(wrapped, stats[0], stats[1], stats[2], stats[3], stats[4])
    return (value, pullback(jnp.ones_like(value)))

def pair_moments(inst_rows, lag_rows):
    sum_inst = lax.optimization_barrier(jnp.sum(inst_rows.astype(jnp.float32), axis=0))
    sum_lag = lax.optimization_barrier(jnp.sum(lag_rows.astype(jnp.float32), axis=0))
    cov_inst = jnp.dot(inst_rows.T.astype(jnp.float32), inst_rows.astype(jnp.float32), preferred_element_type=jnp.float32)
    cov_cross = jnp.dot(inst_rows.T.astype(jnp.float32), lag_rows.astype(jnp.float32), preferred_element_type=jnp.float32)
    cov_lag = jnp.dot(lag_rows.T.astype(jnp.float32), lag_rows.astype(jnp.float32), preferred_element_type=jnp.float32)
    return (sum_inst, sum_lag, cov_inst, cov_cross, cov_lag)

def pair_grads(inst_rows, lag_rows, grads):
    g_si, g_sl, g_ii, g_il, g_ll = grads
    d_inst = g_si[None, :] + jnp.dot(inst_rows, g_ii + g_ii.T, precision=PRECISE) + jnp.dot(lag_rows, g_il.T, precision=PRECISE)
    d_lag = g_sl[None, :] + jnp.dot(inst_rows, g_il, precision=PRECISE) + jnp.dot(lag_rows, g_ll + g_ll.T, precision=PRECISE)
    return (d_inst, d_lag)

def reference(archive, w_first, b_first, w_second, pair_table):
    pre_act = jnp.dot(archive.astype(jnp.float32), w_first.astype(jnp.float32), preferred_element_type=jnp.float32) + b_first
    hidden = jax.nn.elu(pre_act).astype(jnp.bfloat16)
    features = jnp.dot(hidden.astype(jnp.float32), w_second.astype(jnp.float32), preferred_element_type=jnp.float32).astype(jnp.bfloat16)
    steps_len = archive.shape[0] // TRAJS
    inst_index = (pair_table[:, 2] * steps_len + pair_table[:, 0]).astype(jnp.int32)
    lag_index = (pair_table[:, 2] * steps_len + pair_table[:, 1]).astype(jnp.int32)
    inst_rows = jnp.take(features, inst_index, axis=0)
    lag_rows = jnp.take(features, lag_index, axis=0)
    stats = pair_moments(inst_rows, lag_rows)
    score, grads = score_grads(stats, float(pair_table.shape[0]))
    d_inst, d_lag = pair_grads(inst_rows.astype(jnp.float32), lag_rows.astype(jnp.float32), grads)
    frame_terms = jnp.zeros(features.shape, jnp.float32).at[inst_index].add(d_inst).at[lag_index].add(d_lag)
    frame_grad = frame_terms.astype(jnp.bfloat16)
    grad_second = jnp.dot(hidden.T.astype(jnp.float32), frame_grad.astype(jnp.float32), preferred_element_type=jnp.float32)
    slope = jnp.where(pre_act > 0, 1.0, jnp.exp(jnp.minimum(pre_act, 0.0)))
    d_pre = (jnp.dot(frame_grad.astype(jnp.float32), w_second.T.astype(jnp.float32), preferred_element_type=jnp.float32) * slope).astype(jnp.bfloat16)
    grad_bias = lax.optimization_barrier(jnp.sum(d_pre.astype(jnp.float32), axis=0))
    grad_first = jnp.dot(archive.T.astype(jnp.float32), d_pre.astype(jnp.float32), preferred_element_type=jnp.float32)
    return (score.reshape(1), grad_first, grad_bias, grad_second)
```

```python
import functools

import jax
import jax.numpy as jnp
from jax import lax
from jax.experimental import pallas as pl
from jax.experimental.pallas import tpu as pltpu
from jax.sharding import PartitionSpec as P

TRAJS = 4
LAG_PARTS = 32
EPS = 0.001
HIGHEST = lax.Precision.HIGHEST
MIB = 1 << 20


def elu(v):
    return jnp.where(v > 0, v, jnp.exp(jnp.minimum(v, 0.0)) - 1.0)


def exchange_kernel(
    n,
    archive,
    w_first,
    b_first,
    w_second,
    count,
    feats,
    pre_all,
    count_out,
    out_half,
    in_half,
    own_half,
    send_buf,
    recv_buf,
    count_in,
    count_all,
    pair_send,
    pair_recv,
    sum_send,
    sum_recv,
    cnt_send,
    cnt_recv,
    feat_send,
    feat_recv,
    pre_send,
    pre_recv,
):
    frames, hid = archive.shape[0], w_first.shape[1]
    half = frames // 2
    chips = n // 2
    rows = frames // n
    me = lax.axis_index("rep")
    core = lax.rem(me, 2)
    chip = me // 2
    partner = me + 1 - 2 * core

    def to(device):
        return {"rep": device}

    def peer_of(d):
        other = lax.rem(chip + d, chips)
        return other, other * 2 + core

    barrier = pltpu.get_barrier_semaphore()
    pl.semaphore_signal(barrier, inc=1, device_id=to(partner), device_id_type=pl.DeviceIdType.MESH)

    @pl.loop(1, chips)
    def _(d):
        pl.semaphore_signal(
            barrier, inc=1, device_id=to(peer_of(d)[1]), device_id_type=pl.DeviceIdType.MESH
        )

    def remote(src, dst, send, recv, device):
        return pltpu.make_async_remote_copy(
            src_ref=src,
            dst_ref=dst,
            send_sem=send,
            recv_sem=recv,
            device_id=to(device),
            device_id_type=pl.DeviceIdType.MESH,
        )

    tile = 256

    def matmul(row0, nrows, dst, dst0):
        @pl.loop(0, hid // tile)
        def _(t):
            cols = pl.ds(pl.multiple_of(t * tile, tile), tile)
            dst[pl.ds(dst0, nrows), cols] = jnp.dot(
                archive[pl.ds(pl.multiple_of(row0, 32), nrows), :],
                w_first[:, cols],
                preferred_element_type=jnp.float32,
            )

    piece = half // 2
    pieces = []
    for i in range(2):
        matmul((1 - core) * half + i * piece, piece, out_half, i * piece)
        if i == 0:
            pl.semaphore_wait(barrier, chips)
            cnt_copy = remote(count, count_in, cnt_send.at[chips], cnt_recv.at[chips], partner)
            cnt_copy.start()
        part = pl.ds(i * piece, piece)
        copy = remote(out_half.at[part], in_half.at[part], pair_send.at[i], pair_recv.at[i], partner)
        copy.start()
        pieces.append(copy)
    matmul(core * half, half, own_half, 0)

    cnt_copy.wait()
    count_all[chip] = count[...] + count_in[...]

    def cnt_remote(d):
        return remote(
            count_all.at[chip], count_all.at[chip], cnt_send.at[d], cnt_recv.at[chip], peer_of(d)[1]
        )

    @pl.loop(1, chips)
    def _(d):
        cnt_remote(d).start()

    for copy in pieces:
        copy.wait()

    def sum_remote(d):
        other, device = peer_of(d)
        return remote(
            send_buf.at[other], recv_buf.at[chip], sum_send.at[d], sum_recv.at[chip], device
        )

    @pl.loop(1, chips)
    def _(d):
        other = peer_of(d)[0]
        block = pl.ds(pl.multiple_of(other * rows, rows), rows)
        send_buf[other] = (own_half[block, :] + in_half[block, :]).astype(jnp.bfloat16)
        sum_remote(d).start()

    mine = pl.ds(pl.multiple_of(chip * rows, rows), rows)
    own_half[mine, :] = own_half[mine, :] + in_half[mine, :] + b_first[...]

    @pl.loop(1, chips)
    def _(d):
        other = peer_of(d)[0]
        remote(send_buf.at[other], recv_buf.at[other], sum_send.at[d], sum_recv.at[other], partner).wait_recv()
        own_half[mine, :] = own_half[mine, :] + recv_buf[other].astype(jnp.float32)

    pre_act = own_half[mine, :]
    hidden = elu(pre_act).astype(jnp.bfloat16)
    place = pl.ds(pl.multiple_of(core * half + chip * rows, rows), rows)
    feats[place, :] = jnp.dot(hidden, w_second[...], preferred_element_type=jnp.float32).astype(
        jnp.bfloat16
    )

    def gather_remote(buf, send, recv, d):
        return remote(buf.at[place], buf.at[place], send.at[d], recv.at[chip], peer_of(d)[1])

    @pl.loop(1, chips)
    def _(d):
        gather_remote(feats, feat_send, feat_recv, d).start()

    pre_all[place, :] = pre_act.astype(jnp.bfloat16)

    @pl.loop(1, chips)
    def _(d):
        gather_remote(pre_all, pre_send, pre_recv, d).start()

    def forward(buf, send, recv):
        @pl.loop(1, chips)
        def _(d):
            other = peer_of(d)[0]
            theirs = pl.ds(pl.multiple_of(core * half + other * rows, rows), rows)
            remote(buf.at[theirs], buf.at[theirs], send.at[d], recv.at[other], partner).wait_recv()

        side = pl.ds(pl.multiple_of(core * half, half), half)
        copy = remote(buf.at[side], buf.at[side], send.at[chips], recv.at[chips], partner)
        copy.start()
        return copy

    feat_copy = forward(feats, feat_send, feat_recv)

    @pl.loop(1, chips)
    def _(d):
        other = peer_of(d)[0]
        remote(count_all.at[other], count_all.at[other], cnt_send.at[d], cnt_recv.at[other], partner).wait_recv()

    count_out[...] = jnp.sum(count_all[...], axis=0)
    pre_copy = forward(pre_all, pre_send, pre_recv)
    feat_copy.wait()
    pre_copy.wait()

    @pl.loop(1, chips)
    def _(d):
        cnt_remote(d).wait_send()
        sum_remote(d).wait_send()
        gather_remote(feats, feat_send, feat_recv, d).wait_send()
        gather_remote(pre_all, pre_send, pre_recv, d).wait_send()


def exchange(n, archive, w_first, b_first, w_second, count):
    frames, hid, feat = archive.shape[0], w_first.shape[1], w_second.shape[1]
    half, chips, rows = frames // 2, n // 2, frames // n
    vmem = pl.BlockSpec(memory_space=pltpu.VMEM)
    dma = pltpu.SemaphoreType.DMA
    return pl.pallas_call(
        functools.partial(exchange_kernel, n),
        out_shape=(
            jax.ShapeDtypeStruct((frames, feat), jnp.bfloat16),
            jax.ShapeDtypeStruct((frames, hid), jnp.bfloat16),
            jax.ShapeDtypeStruct(count.shape, jnp.float32),
        ),
        in_specs=[vmem] * 5,
        out_specs=(vmem, vmem, vmem),
        scratch_shapes=[
            pltpu.VMEM((half, hid), jnp.float32),
            pltpu.VMEM((half, hid), jnp.float32),
            pltpu.VMEM((half, hid), jnp.float32),
            pltpu.VMEM((chips, rows, hid), jnp.bfloat16),
            pltpu.VMEM((chips, rows, hid), jnp.bfloat16),
            pltpu.VMEM(count.shape, jnp.float32),
            pltpu.VMEM((chips,) + count.shape, jnp.float32),
            dma((2,)),
            dma((2,)),
            dma((chips,)),
            dma((chips,)),
            dma((chips + 1,)),
            dma((chips + 1,)),
            dma((chips + 1,)),
            dma((chips + 1,)),
            dma((chips + 1,)),
            dma((chips + 1,)),
        ],
        compiler_params=pltpu.CompilerParams(
            collective_id=0, has_side_effects=True, vmem_limit_bytes=52 * MIB
        ),
        name="exchange",
    )(archive, w_first, b_first, w_second, count)


def mm(a, b, dims=((1,), (0,))):
    return lax.dot_general(
        a, b, (dims, ((), ())), precision=HIGHEST, preferred_element_type=jnp.float32
    )


TN = ((0,), (0,))
NT = ((1,), (1,))


def score_kernel(tau, total_pairs, feats, count, score, frame_grad):
    frames, feat = feats.shape
    columns = jnp.concatenate(
        [count[...], jnp.zeros((128 - count.shape[0], 128), jnp.float32)], axis=0
    ).T
    n = jnp.concatenate([columns[:, i : i + 1] for i in range(frames // 128)], axis=0)
    first = feats[...].astype(jnp.float32)
    later = jnp.concatenate([first[tau:], first[:tau]], axis=0)
    scale = 1.0 / total_pairs
    x0 = first - jnp.sum(first * n, axis=0, keepdims=True) * scale
    xt = later - jnp.sum(later * n, axis=0, keepdims=True) * scale
    n = n * scale
    x0n = x0 * n
    xtn = xt * n
    eye = (
        lax.broadcasted_iota(jnp.int32, (feat, feat), 0)
        == lax.broadcasted_iota(jnp.int32, (feat, feat), 1)
    ).astype(jnp.float32)
    c00 = mm(x0n, x0, TN) + EPS * eye
    ctt = mm(xtn, xt, TN) + EPS * eye
    c0t = mm(x0n, xt, TN)
    top0 = jnp.max(jnp.sum(jnp.abs(c00), axis=0, keepdims=True), axis=1, keepdims=True)
    topt = jnp.max(jnp.sum(jnp.abs(ctt), axis=0, keepdims=True), axis=1, keepdims=True)
    c00 = c00 / top0
    ctt = ctt / topt
    low = EPS / jnp.max(jnp.maximum(top0, topt))

    def gain(low):
        return 4.0 / jnp.square(1.0 + low)

    a = gain(low) * ((1.0 + low) * eye - c00)
    b = gain(low) * ((1.0 + low) * eye - ctt)

    def step(carry):
        low, a, b = carry
        g = gain(low)
        s = 1.0 + low
        ra = s * eye - mm(c00, a)
        rb = s * eye - mm(ctt, b)
        return (jnp.minimum(g * low, 1.0), g * mm(a, ra), g * mm(b, rb))

    _, a, b = lax.while_loop(lambda carry: carry[0] < 1.0 - 2e-6, step, (gain(low) * low, a, b))
    a = a / top0
    b = b / topt
    u = mm(a, c0t)
    v = mm(c0t, b)
    k = mm(u, b)
    score[...] = jnp.broadcast_to(1.0 + jnp.sum(u * v), score.shape)
    g00 = -2.0 * mm(k, u, NT)
    gtt = -2.0 * mm(k, v, TN)
    k = 2.0 * k
    d0 = n * (mm(x0, g00) + mm(xt, k, NT))
    dt = n * (mm(x0, k) + mm(xt, gtt))
    dt = jnp.concatenate([dt[frames - tau :], dt[: frames - tau]], axis=0)
    frame_grad[...] = (d0 + dt).astype(jnp.bfloat16)


def score_and_grad(tau, total_pairs, feats, count):
    vmem = pl.BlockSpec(memory_space=pltpu.VMEM)
    return pl.pallas_call(
        functools.partial(score_kernel, tau, total_pairs),
        out_shape=(
            jax.ShapeDtypeStruct((8, 128), jnp.float32),
            jax.ShapeDtypeStruct(feats.shape, jnp.bfloat16),
        ),
        in_specs=[vmem] * 2,
        out_specs=(vmem, vmem),
        compiler_params=pltpu.CompilerParams(vmem_limit_bytes=52 * MIB),
        name="score",
    )(feats, count)


def per_device(n, archive, w_first, b_first, w_second, pair_table):
    frames_total = archive.shape[0]
    steps_len = frames_total // TRAJS
    tau = frames_total // LAG_PARTS
    total_pairs = float(pair_table.shape[0] * n)
    inst_index = pair_table[:, 2] * steps_len + pair_table[:, 0]
    count_rows = max(8, frames_total // 128)
    frame_ids = lax.broadcasted_iota(jnp.int32, (count_rows, 128), 0) * 128 + lax.broadcasted_iota(
        jnp.int32, (count_rows, 128), 1
    )
    count = jnp.sum(
        (inst_index[:, None, None] == frame_ids[None]).astype(jnp.float32), axis=0
    )
    feats, pre_act, count = exchange(n, archive, w_first, b_first[None, :], w_second, count)
    score, frame_grad = score_and_grad(tau, total_pairs, feats, count)
    pre_act = pre_act.astype(jnp.float32)
    hidden = elu(pre_act).astype(jnp.bfloat16)
    slope = jnp.where(pre_act > 0, 1.0, jnp.exp(jnp.minimum(pre_act, 0.0)))
    d_pre = (jnp.dot(frame_grad, w_second.T, preferred_element_type=jnp.float32) * slope).astype(
        jnp.bfloat16
    )
    grad_second = jnp.dot(hidden.T, frame_grad, preferred_element_type=jnp.float32)
    grad_bias = jnp.sum(d_pre.astype(jnp.float32), axis=0)
    grad_first = lax.dot_general(
        archive, d_pre, (((0,), (0,)), ((), ())), preferred_element_type=jnp.float32
    )
    return (score[0, :1], grad_first, grad_bias, grad_second)


def solution(mesh):
    placed = (
        P("group", "rep"),
        P(("group", "rep"), None),
        P("group"),
        P("group", None),
        P(("group", "rep"), None),
    )
    return jax.shard_map(
        functools.partial(per_device, mesh.shape["rep"]),
        mesh=mesh,
        in_specs=placed,
        out_specs=(P("group"), P(("group", "rep"), None), P("group"), P("group", None)),
        check_vma=False,
    )
```

```python
import functools

import jax
import jax.numpy as jnp
from jax import lax
from jax.experimental import pallas as pl
from jax.experimental.pallas import tpu as pltpu
from jax.sharding import PartitionSpec as P

TRAJS = 4
LAG_PARTS = 32
EPS = 0.001
MIB = 1 << 20


def elu(v):
    return jnp.where(v > 0, v, jnp.exp(jnp.minimum(v, 0.0)) - 1.0)


def exchange_kernel(
    n,
    archive,
    w_first,
    b_first,
    w_second,
    count,
    feats,
    pre_all,
    count_out,
    out_half,
    in_half,
    own_half,
    send_buf,
    recv_buf,
    count_in,
    count_all,
    pair_send,
    pair_recv,
    sum_send,
    sum_recv,
    cnt_send,
    cnt_recv,
    feat_send,
    feat_recv,
    pre_send,
    pre_recv,
):
    frames, hid = archive.shape[0], w_first.shape[1]
    half = frames // 2
    chips = n // 2
    rows = frames // n
    me = lax.axis_index("rep")
    core = lax.rem(me, 2)
    chip = me // 2
    partner = me + 1 - 2 * core

    def to(device):
        return {"rep": device}

    def peer_of(d):
        other = lax.rem(chip + d, chips)
        return other, other * 2 + core

    barrier = pltpu.get_barrier_semaphore()
    pl.semaphore_signal(barrier, inc=1, device_id=to(partner), device_id_type=pl.DeviceIdType.MESH)

    @pl.loop(1, chips)
    def _(d):
        pl.semaphore_signal(
            barrier, inc=1, device_id=to(peer_of(d)[1]), device_id_type=pl.DeviceIdType.MESH
        )

    def remote(src, dst, send, recv, device):
        return pltpu.make_async_remote_copy(
            src_ref=src,
            dst_ref=dst,
            send_sem=send,
            recv_sem=recv,
            device_id=to(device),
            device_id_type=pl.DeviceIdType.MESH,
        )

    tile = 256

    def matmul(row0, nrows, dst, dst0):
        @pl.loop(0, hid // tile)
        def _(t):
            cols = pl.ds(pl.multiple_of(t * tile, tile), tile)
            dst[pl.ds(dst0, nrows), cols] = jnp.dot(
                archive[pl.ds(pl.multiple_of(row0, 32), nrows), :],
                w_first[:, cols],
                preferred_element_type=jnp.float32,
            )

    piece = half // 2
    side_chips = chips // 2
    side = chip // side_chips

    def sum_remote(other):
        return remote(
            send_buf.at[other],
            recv_buf.at[chip],
            sum_send.at[other],
            sum_recv.at[chip],
            other * 2 + core,
        )

    def send_sum(other):
        block = pl.ds(pl.multiple_of(other * rows, rows), rows)
        send_buf[other] = (own_half[block, :] + in_half[block, :]).astype(jnp.bfloat16)
        sum_remote(other).start()

    def partner_piece(which, index):
        start = pl.multiple_of(which * piece, 32)
        matmul((1 - core) * half + start, piece, out_half, start)
        if index == 0:
            pl.semaphore_wait(barrier, chips)
        part = pl.ds(start, piece)
        copy = remote(
            out_half.at[part], in_half.at[part], pair_send.at[index], pair_recv.at[index], partner
        )
        copy.start()
        return copy

    def own_piece(which):
        start = pl.multiple_of(which * piece, 32)
        matmul(core * half + start, piece, own_half, start)

    far_copy = partner_piece(1 - side, 0)
    own_piece(1 - side)
    near_copy = partner_piece(side, 1)
    far_copy.wait_recv()

    @pl.loop(0, side_chips)
    def _(j):
        send_sum((1 - side) * side_chips + lax.rem(chip + j, side_chips))

    cnt_copy = remote(count, count_in, cnt_send.at[chips], cnt_recv.at[chips], partner)
    cnt_copy.start()
    own_piece(side)
    near_copy.wait_recv()

    @pl.loop(1, side_chips)
    def _(j):
        send_sum(side * side_chips + lax.rem(chip + j, side_chips))

    cnt_copy.wait()
    count_all[chip] = count[...] + count_in[...]

    def cnt_remote(d):
        return remote(
            count_all.at[chip], count_all.at[chip], cnt_send.at[d], cnt_recv.at[chip], peer_of(d)[1]
        )

    @pl.loop(1, chips)
    def _(d):
        cnt_remote(d).start()

    far_copy.wait_send()
    near_copy.wait_send()

    mine = pl.ds(pl.multiple_of(chip * rows, rows), rows)
    own_half[mine, :] = own_half[mine, :] + in_half[mine, :] + b_first[...]

    @pl.loop(1, chips)
    def _(d):
        other = peer_of(d)[0]
        remote(send_buf.at[other], recv_buf.at[other], sum_send.at[other], sum_recv.at[other], partner).wait_recv()
        own_half[mine, :] = own_half[mine, :] + recv_buf[other].astype(jnp.float32)

    pre_act = own_half[mine, :]
    hidden = elu(pre_act).astype(jnp.bfloat16)
    place = pl.ds(pl.multiple_of(core * half + chip * rows, rows), rows)
    feats[place, :] = jnp.dot(hidden, w_second[...], preferred_element_type=jnp.float32).astype(
        jnp.bfloat16
    )

    def gather_remote(buf, send, recv, d):
        return remote(buf.at[place], buf.at[place], send.at[d], recv.at[chip], peer_of(d)[1])

    @pl.loop(1, chips)
    def _(d):
        gather_remote(feats, feat_send, feat_recv, d).start()

    pre_all[place, :] = pre_act.astype(jnp.bfloat16)

    @pl.loop(1, chips)
    def _(d):
        gather_remote(pre_all, pre_send, pre_recv, d).start()

    def forward(buf, send, recv):
        @pl.loop(1, chips)
        def _(d):
            other = peer_of(d)[0]
            theirs = pl.ds(pl.multiple_of(core * half + other * rows, rows), rows)
            remote(buf.at[theirs], buf.at[theirs], send.at[d], recv.at[other], partner).wait_recv()

        side = pl.ds(pl.multiple_of(core * half, half), half)
        copy = remote(buf.at[side], buf.at[side], send.at[chips], recv.at[chips], partner)
        copy.start()
        return copy

    feat_copy = forward(feats, feat_send, feat_recv)

    @pl.loop(1, chips)
    def _(d):
        other = peer_of(d)[0]
        remote(count_all.at[other], count_all.at[other], cnt_send.at[d], cnt_recv.at[other], partner).wait_recv()

    count_out[...] = jnp.sum(count_all[...], axis=0)
    pre_copy = forward(pre_all, pre_send, pre_recv)
    feat_copy.wait()
    pre_copy.wait()

    @pl.loop(1, chips)
    def _(d):
        cnt_remote(d).wait_send()
        sum_remote(peer_of(d)[0]).wait_send()
        gather_remote(feats, feat_send, feat_recv, d).wait_send()
        gather_remote(pre_all, pre_send, pre_recv, d).wait_send()


def exchange(n, archive, w_first, b_first, w_second, count):
    frames, hid, feat = archive.shape[0], w_first.shape[1], w_second.shape[1]
    half, chips, rows = frames // 2, n // 2, frames // n
    vmem = pl.BlockSpec(memory_space=pltpu.VMEM)
    dma = pltpu.SemaphoreType.DMA
    return pl.pallas_call(
        functools.partial(exchange_kernel, n),
        out_shape=(
            jax.ShapeDtypeStruct((frames, feat), jnp.bfloat16),
            jax.ShapeDtypeStruct((frames, hid), jnp.bfloat16),
            jax.ShapeDtypeStruct(count.shape, jnp.float32),
        ),
        in_specs=[vmem] * 5,
        out_specs=(vmem, vmem, vmem),
        scratch_shapes=[
            pltpu.VMEM((half, hid), jnp.float32),
            pltpu.VMEM((half, hid), jnp.float32),
            pltpu.VMEM((half, hid), jnp.float32),
            pltpu.VMEM((chips, rows, hid), jnp.bfloat16),
            pltpu.VMEM((chips, rows, hid), jnp.bfloat16),
            pltpu.VMEM(count.shape, jnp.float32),
            pltpu.VMEM((chips,) + count.shape, jnp.float32),
            dma((2,)),
            dma((2,)),
            dma((chips,)),
            dma((chips,)),
            dma((chips + 1,)),
            dma((chips + 1,)),
            dma((chips + 1,)),
            dma((chips + 1,)),
            dma((chips + 1,)),
            dma((chips + 1,)),
        ],
        compiler_params=pltpu.CompilerParams(
            collective_id=0, has_side_effects=True, vmem_limit_bytes=52 * MIB
        ),
        name="exchange",
    )(archive, w_first, b_first, w_second, count)


def mm(a, b, dims=((1,), (0,))):
    a_top, b_top = a.astype(jnp.bfloat16), b.astype(jnp.bfloat16)
    a_rest = (a - a_top.astype(jnp.float32)).astype(jnp.bfloat16)
    b_rest = (b - b_top.astype(jnp.float32)).astype(jnp.bfloat16)

    def dot(x, y):
        return lax.dot_general(x, y, (dims, ((), ())), preferred_element_type=jnp.float32)

    return dot(a_top, b_top) + (dot(a_top, b_rest) + dot(a_rest, b_top))


TN = ((0,), (0,))
NT = ((1,), (1,))


def score_into(tau, total_pairs, feats, count, score, frame_grad):
    frames, feat = feats.shape
    columns = jnp.concatenate(
        [count[...], jnp.zeros((128 - count.shape[0], 128), jnp.float32)], axis=0
    ).T
    n = jnp.concatenate([columns[:, i : i + 1] for i in range(frames // 128)], axis=0)
    first = feats[...].astype(jnp.float32)
    later = jnp.concatenate([first[tau:], first[:tau]], axis=0)
    scale = 1.0 / total_pairs
    x0 = first - jnp.sum(first * n, axis=0, keepdims=True) * scale
    xt = later - jnp.sum(later * n, axis=0, keepdims=True) * scale
    n = n * scale
    x0n = x0 * n
    xtn = xt * n
    eye = (
        lax.broadcasted_iota(jnp.int32, (feat, feat), 0)
        == lax.broadcasted_iota(jnp.int32, (feat, feat), 1)
    ).astype(jnp.float32)
    c00 = mm(x0n, x0, TN) + EPS * eye
    ctt = mm(xtn, xt, TN) + EPS * eye
    c0t = mm(x0n, xt, TN)
    top0 = jnp.max(jnp.sum(jnp.abs(c00), axis=0, keepdims=True), axis=1, keepdims=True)
    topt = jnp.max(jnp.sum(jnp.abs(ctt), axis=0, keepdims=True), axis=1, keepdims=True)
    c00 = c00 / top0
    ctt = ctt / topt
    low = EPS / jnp.max(jnp.maximum(top0, topt))

    def gain(low):
        return 4.0 / jnp.square(1.0 + low)

    a = gain(low) * ((1.0 + low) * eye - c00)
    b = gain(low) * ((1.0 + low) * eye - ctt)

    def step(carry):
        low, a, b = carry
        g = gain(low)
        s = 1.0 + low
        ra = s * eye - mm(c00, a)
        rb = s * eye - mm(ctt, b)
        return (jnp.minimum(g * low, 1.0), g * mm(a, ra), g * mm(b, rb))

    _, a, b = lax.while_loop(lambda carry: carry[0] < 1.0 - 2e-6, step, (gain(low) * low, a, b))
    a = a / top0
    b = b / topt
    u = mm(a, c0t)
    v = mm(c0t, b)
    k = mm(u, b)
    score[...] = jnp.broadcast_to(1.0 + jnp.sum(u * v), score.shape)
    g00 = -2.0 * mm(k, u, NT)
    gtt = -2.0 * mm(k, v, TN)
    k = 2.0 * k
    d0 = n * (mm(x0, g00) + mm(xt, k, NT))
    dt = n * (mm(x0, k) + mm(xt, gtt))
    dt = jnp.concatenate([dt[frames - tau :], dt[: frames - tau]], axis=0)
    frame_grad[...] = (d0 + dt).astype(jnp.bfloat16)


def finish_kernel(
    tau,
    total_pairs,
    feats,
    count,
    pre_act,
    w_second,
    archive,
    score,
    grad_first,
    grad_bias,
    grad_second,
    frame_grad,
    d_pre,
):
    tile = feats.shape[1]

    @pl.when(pl.program_id(0) == 0)
    def _():
        score_into(tau, total_pairs, feats, count, score, frame_grad)

        @pl.loop(0, d_pre.shape[1] // tile)
        def _(t):
            part = pl.ds(pl.multiple_of(t * tile, tile), tile)
            pre = pre_act[:, part].astype(jnp.float32)
            low_exp = jnp.exp(jnp.minimum(pre, 0.0))
            positive = pre > 0
            hidden = jnp.where(positive, pre, low_exp - 1.0).astype(jnp.bfloat16)
            back = lax.dot_general(
                frame_grad[...],
                w_second[part, :],
                (NT, ((), ())),
                preferred_element_type=jnp.float32,
            )
            grad = (back * jnp.where(positive, 1.0, low_exp)).astype(jnp.bfloat16)
            d_pre[:, part] = grad
            grad_bias[:, part] = jnp.sum(grad.astype(jnp.float32), axis=0, keepdims=True)
            grad_second[part, :] = lax.dot_general(
                hidden, frame_grad[...], (TN, ((), ())), preferred_element_type=jnp.float32
            )

    grad_first[...] = lax.dot_general(
        archive[...], d_pre[...], (TN, ((), ())), preferred_element_type=jnp.float32
    )


def finish(tau, total_pairs, feats, count, pre_act, w_second, archive):
    frames, feat = feats.shape
    hid, field = w_second.shape[0], archive.shape[1]
    tile = 256

    def whole(shape):
        return pl.BlockSpec(shape, lambda i: (0,) * len(shape))

    return pl.pallas_call(
        functools.partial(finish_kernel, tau, total_pairs),
        grid=(field // tile,),
        out_shape=(
            jax.ShapeDtypeStruct((8, 128), jnp.float32),
            jax.ShapeDtypeStruct((field, hid), jnp.float32),
            jax.ShapeDtypeStruct((1, hid), jnp.float32),
            jax.ShapeDtypeStruct((hid, feat), jnp.float32),
        ),
        in_specs=[
            whole(feats.shape),
            whole(count.shape),
            whole(pre_act.shape),
            whole(w_second.shape),
            pl.BlockSpec((frames, tile), lambda i: (0, i)),
        ],
        out_specs=(
            whole((8, 128)),
            pl.BlockSpec((tile, hid), lambda i: (i, 0)),
            whole((1, hid)),
            whole((hid, feat)),
        ),
        scratch_shapes=[
            pltpu.VMEM((frames, feat), jnp.bfloat16),
            pltpu.VMEM((frames, hid), jnp.bfloat16),
        ],
        compiler_params=pltpu.CompilerParams(vmem_limit_bytes=52 * MIB),
        name="finish",
    )(feats, count, pre_act, w_second, archive)


def per_device(n, archive, w_first, b_first, w_second, pair_table):
    frames_total = archive.shape[0]
    steps_len = frames_total // TRAJS
    tau = frames_total // LAG_PARTS
    total_pairs = float(pair_table.shape[0] * n)
    inst_index = pair_table[:, 2] * steps_len + pair_table[:, 0]
    count_rows = max(8, frames_total // 128)
    frame_ids = lax.broadcasted_iota(jnp.int32, (count_rows, 128), 0) * 128 + lax.broadcasted_iota(
        jnp.int32, (count_rows, 128), 1
    )
    count = jnp.sum(
        (inst_index[:, None, None] == frame_ids[None]).astype(jnp.float32), axis=0
    )
    feats, pre_act, count = exchange(n, archive, w_first, b_first[None, :], w_second, count)
    score, grad_first, grad_bias, grad_second = finish(
        tau, total_pairs, feats, count, pre_act, w_second, archive
    )
    return (score[0, :1], grad_first, grad_bias[0], grad_second)


def solution(mesh):
    placed = (
        P("group", "rep"),
        P(("group", "rep"), None),
        P("group"),
        P("group", None),
        P(("group", "rep"), None),
    )
    return jax.shard_map(
        functools.partial(per_device, mesh.shape["rep"]),
        mesh=mesh,
        in_specs=placed,
        out_specs=(P("group"), P(("group", "rep"), None), P("group"), P("group", None)),
        check_vma=False,
    )
```

```python
import functools

import jax
import jax.numpy as jnp
from jax import lax
from jax.experimental import pallas as pl
from jax.experimental.pallas import tpu as pltpu
from jax.sharding import PartitionSpec as P

TRAJS = 4
LAG_PARTS = 32
EPS = 0.001
MIB = 1 << 20


def elu(v):
    return jnp.where(v > 0, v, jnp.exp(jnp.minimum(v, 0.0)) - 1.0)


def exchange_kernel(
    n,
    tau,
    total_pairs,
    archive,
    w_first,
    b_hbm,
    w_second_hbm,
    index,
    feats,
    pre_all,
    weight,
    c00,
    ctt,
    c0t,
    inv0,
    invt,
    info,
    b_first,
    w_second,
    load_sem,
    out_half,
    in_half,
    own_half,
    send_buf,
    recv_buf,
    index_all,
    pair_send,
    pair_recv,
    sum_send,
    sum_recv,
    cnt_send,
    cnt_recv,
    feat_send,
    feat_recv,
    pre_send,
    pre_recv,
):
    frames, hid = archive.shape[0], w_first.shape[1]
    half = frames // 2
    chips = n // 2
    rows = frames // n
    me = lax.axis_index("rep")
    core = lax.rem(me, 2)
    chip = me // 2
    partner = me + 1 - 2 * core

    def to(device):
        return {"rep": device}

    def peer_of(d):
        other = lax.rem(chip + d, chips)
        return other, other * 2 + core

    loads = [
        pltpu.make_async_copy(b_hbm, b_first, load_sem.at[0]),
        pltpu.make_async_copy(w_second_hbm, w_second, load_sem.at[1]),
    ]
    for load in loads:
        load.start()
    barrier = pltpu.get_barrier_semaphore()
    pl.semaphore_signal(barrier, inc=1, device_id=to(partner), device_id_type=pl.DeviceIdType.MESH)

    @pl.loop(1, chips)
    def _(d):
        pl.semaphore_signal(
            barrier, inc=1, device_id=to(peer_of(d)[1]), device_id_type=pl.DeviceIdType.MESH
        )

    def remote(src, dst, send, recv, device):
        return pltpu.make_async_remote_copy(
            src_ref=src,
            dst_ref=dst,
            send_sem=send,
            recv_sem=recv,
            device_id=to(device),
            device_id_type=pl.DeviceIdType.MESH,
        )

    tile = 256

    def matmul(row0, nrows, dst, dst0):
        @pl.loop(0, hid // tile)
        def _(t):
            cols = pl.ds(pl.multiple_of(t * tile, tile), tile)
            dst[pl.ds(dst0, nrows), cols] = jnp.dot(
                archive[pl.ds(pl.multiple_of(row0, 32), nrows), :],
                w_first[:, cols],
                preferred_element_type=jnp.float32,
            )

    piece = half // 2
    side_chips = chips // 2
    side = chip // side_chips

    def sum_remote(other):
        return remote(
            send_buf.at[other],
            recv_buf.at[chip],
            sum_send.at[other],
            sum_recv.at[chip],
            other * 2 + core,
        )

    def send_sum(other):
        block = pl.ds(pl.multiple_of(other * rows, rows), rows)
        send_buf[other] = (own_half[block, :] + in_half[block, :]).astype(jnp.bfloat16)
        sum_remote(other).start()

    def partner_piece(which, index):
        start = pl.multiple_of(which * piece, 32)
        matmul((1 - core) * half + start, piece, out_half, start)
        if index == 0:
            pl.semaphore_wait(barrier, chips)
        part = pl.ds(start, piece)
        copy = remote(
            out_half.at[part], in_half.at[part], pair_send.at[index], pair_recv.at[index], partner
        )
        copy.start()
        return copy

    def own_piece(which):
        start = pl.multiple_of(which * piece, 32)
        matmul(core * half + start, piece, own_half, start)

    far_copy = partner_piece(1 - side, 0)
    own_piece(1 - side)
    near_copy = partner_piece(side, 1)
    far_copy.wait_recv()

    @pl.loop(0, side_chips)
    def _(j):
        send_sum((1 - side) * side_chips + lax.rem(chip + j, side_chips))

    index_all[me] = jnp.broadcast_to(index[...], index_all.shape[1:])
    cnt_copy = remote(
        index_all.at[me], index_all.at[me], cnt_send.at[chips], cnt_recv.at[chips], partner
    )
    cnt_copy.start()
    own_piece(side)
    near_copy.wait_recv()

    @pl.loop(1, side_chips)
    def _(j):
        send_sum(side * side_chips + lax.rem(chip + j, side_chips))

    cnt_copy.wait()
    for load in loads:
        load.wait()

    def cnt_remote(d):
        both = index_all.at[pl.ds(chip * 2, 2)]
        return remote(both, both, cnt_send.at[d], cnt_recv.at[chip], peer_of(d)[1])

    @pl.loop(1, chips)
    def _(d):
        cnt_remote(d).start()

    far_copy.wait_send()
    near_copy.wait_send()

    mine = pl.ds(pl.multiple_of(chip * rows, rows), rows)
    own_half[mine, :] = own_half[mine, :] + in_half[mine, :] + b_first[...]

    @pl.loop(1, chips)
    def _(d):
        other = peer_of(d)[0]
        remote(send_buf.at[other], recv_buf.at[other], sum_send.at[other], sum_recv.at[other], partner).wait_recv()
        own_half[mine, :] = own_half[mine, :] + recv_buf[other].astype(jnp.float32)

    pre_act = own_half[mine, :]
    hidden = elu(pre_act).astype(jnp.bfloat16)
    place = pl.ds(pl.multiple_of(core * half + chip * rows, rows), rows)
    feats[place, :] = jnp.dot(hidden, w_second[...], preferred_element_type=jnp.float32).astype(
        jnp.bfloat16
    )

    def gather_remote(buf, send, recv, d):
        return remote(buf.at[place], buf.at[place], send.at[d], recv.at[chip], peer_of(d)[1])

    @pl.loop(1, chips)
    def _(d):
        gather_remote(feats, feat_send, feat_recv, d).start()

    pre_all[place, :] = pre_act.astype(jnp.bfloat16)

    @pl.loop(1, chips)
    def _(d):
        gather_remote(pre_all, pre_send, pre_recv, d).start()

    def forward(buf, send, recv):
        @pl.loop(1, chips)
        def _(d):
            other = peer_of(d)[0]
            theirs = pl.ds(pl.multiple_of(core * half + other * rows, rows), rows)
            remote(buf.at[theirs], buf.at[theirs], send.at[d], recv.at[other], partner).wait_recv()

        side = pl.ds(pl.multiple_of(core * half, half), half)
        copy = remote(buf.at[side], buf.at[side], send.at[chips], recv.at[chips], partner)
        copy.start()
        return copy

    feat_copy = forward(feats, feat_send, feat_recv)

    @pl.loop(1, chips)
    def _(d):
        other = peer_of(d)[0]
        both = index_all.at[pl.ds(other * 2, 2)]
        remote(both, both, cnt_send.at[d], cnt_recv.at[other], partner).wait_recv()

    @pl.loop(0, frames // 128)
    def _(t):
        ids = t * 128 + lax.broadcasted_iota(jnp.int32, (128, index.shape[1]), 0)

        def add(r, total):
            return total + (index_all[r][0:1, :] == ids).astype(jnp.float32)

        total = lax.fori_loop(0, n, add, jnp.zeros(ids.shape, jnp.float32))
        weight[pl.ds(pl.multiple_of(t * 128, 128), 128), :] = jnp.sum(
            total, axis=1, keepdims=True
        )

    feat_copy.wait()
    start_inverse(tau, total_pairs, feats, weight, c00, ctt, c0t, inv0, invt, info)
    refine(6, c00, ctt, inv0, invt, info)
    pre_copy = forward(pre_all, pre_send, pre_recv)
    refine(3, c00, ctt, inv0, invt, info)
    pre_copy.wait()

    @pl.loop(1, chips)
    def _(d):
        cnt_remote(d).wait_send()
        sum_remote(peer_of(d)[0]).wait_send()
        gather_remote(feats, feat_send, feat_recv, d).wait_send()
        gather_remote(pre_all, pre_send, pre_recv, d).wait_send()


def exchange(n, tau, total_pairs, archive, w_first, b_first, w_second, index):
    frames, hid, feat = archive.shape[0], w_first.shape[1], w_second.shape[1]
    half, chips, rows = frames // 2, n // 2, frames // n
    vmem = pl.BlockSpec(memory_space=pltpu.VMEM)
    hbm = pl.BlockSpec(memory_space=pltpu.HBM)
    dma = pltpu.SemaphoreType.DMA
    square = jax.ShapeDtypeStruct((feat, feat), jnp.float32)
    return pl.pallas_call(
        functools.partial(exchange_kernel, n, tau, total_pairs),
        out_shape=(
            jax.ShapeDtypeStruct((frames, feat), jnp.bfloat16),
            jax.ShapeDtypeStruct((frames, hid), jnp.bfloat16),
            jax.ShapeDtypeStruct((frames, 1), jnp.float32),
            square,
            square,
            square,
            square,
            square,
            jax.ShapeDtypeStruct((8, 128), jnp.float32),
        ),
        in_specs=[vmem, vmem, hbm, hbm, vmem],
        out_specs=(vmem,) * 9,
        scratch_shapes=[
            pltpu.VMEM(b_first.shape, jnp.float32),
            pltpu.VMEM(w_second.shape, jnp.bfloat16),
            dma((2,)),
            pltpu.VMEM((half, hid), jnp.float32),
            pltpu.VMEM((half, hid), jnp.float32),
            pltpu.VMEM((half, hid), jnp.float32),
            pltpu.VMEM((chips, rows, hid), jnp.bfloat16),
            pltpu.VMEM((chips, rows, hid), jnp.bfloat16),
            pltpu.VMEM((n, 8, index.shape[1]), jnp.int32),
            dma((2,)),
            dma((2,)),
            dma((chips,)),
            dma((chips,)),
            dma((chips + 1,)),
            dma((chips + 1,)),
            dma((chips + 1,)),
            dma((chips + 1,)),
            dma((chips + 1,)),
            dma((chips + 1,)),
        ],
        compiler_params=pltpu.CompilerParams(
            collective_id=0, has_side_effects=True, vmem_limit_bytes=40 * MIB
        ),
        name="exchange",
    )(archive, w_first, b_first, w_second, index)


def mm(a, b, dims=((1,), (0,))):
    a_top, b_top = a.astype(jnp.bfloat16), b.astype(jnp.bfloat16)
    a_rest = (a - a_top.astype(jnp.float32)).astype(jnp.bfloat16)
    b_rest = (b - b_top.astype(jnp.float32)).astype(jnp.bfloat16)

    def dot(x, y):
        return lax.dot_general(x, y, (dims, ((), ())), preferred_element_type=jnp.float32)

    return dot(a_top, b_top) + (dot(a_top, b_rest) + dot(a_rest, b_top))


TN = ((0,), (0,))
NT = ((1,), (1,))


def identity(feat):
    return (
        lax.broadcasted_iota(jnp.int32, (feat, feat), 0)
        == lax.broadcasted_iota(jnp.int32, (feat, feat), 1)
    ).astype(jnp.float32)


def centred_rows(tau, scale, feats, n):
    first = feats[...].astype(jnp.float32)
    later = jnp.concatenate([first[tau:], first[:tau]], axis=0)
    x0 = first - jnp.sum(first * n, axis=0, keepdims=True) * scale
    xt = later - jnp.sum(later * n, axis=0, keepdims=True) * scale
    return x0, xt


def gain(low):
    return 4.0 / ((1.0 + low) * (1.0 + low))


def start_inverse(tau, total_pairs, feats, weight, c00, ctt, c0t, inv0, invt, info):
    n = weight[...]
    scale = 1.0 / total_pairs
    x0, xt = centred_rows(tau, scale, feats, n)
    x0n = x0 * (n * scale)
    eye = identity(feats.shape[1])
    first = mm(x0n, x0, TN) + EPS * eye
    c0t[...] = mm(x0n, xt, TN)
    later = mm(xt * (n * scale), xt, TN) + EPS * eye
    top0 = jnp.max(jnp.sum(jnp.abs(first), axis=0, keepdims=True), axis=1, keepdims=True)
    topt = jnp.max(jnp.sum(jnp.abs(later), axis=0, keepdims=True), axis=1, keepdims=True)
    first = first / top0
    later = later / topt
    low = EPS / jnp.maximum(top0, topt)
    c00[...] = first
    ctt[...] = later
    inv0[...] = gain(low) * ((1.0 + low) * eye - first)
    invt[...] = gain(low) * ((1.0 + low) * eye - later)
    info[0:1, :] = jnp.broadcast_to(top0, (1, 128))
    info[1:2, :] = jnp.broadcast_to(topt, (1, 128))
    info[2:3, :] = jnp.broadcast_to(jnp.minimum(gain(low) * low, 1.0), (1, 128))


def newton_step(c00, ctt, inv0, invt, low):
    eye = identity(c00.shape[0])
    a, b = inv0[...], invt[...]
    ra = (1.0 + low) * eye - mm(c00[...], a)
    rb = (1.0 + low) * eye - mm(ctt[...], b)
    inv0[...] = gain(low) * mm(a, ra)
    invt[...] = gain(low) * mm(b, rb)
    return jnp.minimum(gain(low) * low, 1.0)


def refine(steps, c00, ctt, inv0, invt, info):
    @pl.loop(0, steps)
    def _(_):
        low = newton_step(c00, ctt, inv0, invt, info[2:3, 0:1])
        info[2:3, :] = jnp.broadcast_to(low, (1, 128))


def score_into(
    tau, total_pairs, feats, weight, c00, ctt, c0t, start0, startt, info, score, frame_grad, inv0, invt
):
    inv0[...] = start0[...]
    invt[...] = startt[...]
    lax.while_loop(
        lambda low: jnp.max(low) < 1.0 - 2e-6,
        lambda low: newton_step(c00, ctt, inv0, invt, low),
        info[2:3, 0:1],
    )
    a = inv0[...] / info[0:1, 0:1]
    b = invt[...] / info[1:2, 0:1]
    cross = c0t[...]
    u = mm(a, cross)
    v = mm(cross, b)
    k = mm(u, b)
    score[...] = jnp.broadcast_to(1.0 + jnp.sum(u * v), score.shape)
    g00 = -2.0 * mm(k, u, NT)
    gtt = -2.0 * mm(k, v, TN)
    k = 2.0 * k
    n = weight[...]
    scale = 1.0 / total_pairs
    x0, xt = centred_rows(tau, scale, feats, n)
    n = n * scale
    frames = feats.shape[0]
    d0 = n * (mm(x0, g00) + mm(xt, k, NT))
    dt = n * (mm(x0, k) + mm(xt, gtt))
    dt = jnp.concatenate([dt[frames - tau :], dt[: frames - tau]], axis=0)
    frame_grad[...] = (d0 + dt).astype(jnp.bfloat16)


def finish_kernel(
    tau,
    total_pairs,
    feats,
    pre_act,
    weight,
    c00,
    ctt,
    c0t,
    start0,
    startt,
    info,
    w_second,
    archive,
    score,
    grad_first,
    grad_bias,
    grad_second,
    frame_grad,
    d_pre,
    inv0,
    invt,
):
    tile = feats.shape[1]

    @pl.when(pl.program_id(0) == 0)
    def _():
        score_into(
            tau,
            total_pairs,
            feats,
            weight,
            c00,
            ctt,
            c0t,
            start0,
            startt,
            info,
            score,
            frame_grad,
            inv0,
            invt,
        )

        @pl.loop(0, d_pre.shape[1] // tile)
        def _(t):
            part = pl.ds(pl.multiple_of(t * tile, tile), tile)
            pre = pre_act[:, part].astype(jnp.float32)
            low_exp = jnp.exp(jnp.minimum(pre, 0.0))
            positive = pre > 0
            hidden = jnp.where(positive, pre, low_exp - 1.0).astype(jnp.bfloat16)
            back = lax.dot_general(
                frame_grad[...],
                w_second[part, :],
                (NT, ((), ())),
                preferred_element_type=jnp.float32,
            )
            grad = (back * jnp.where(positive, 1.0, low_exp)).astype(jnp.bfloat16)
            d_pre[:, part] = grad
            grad_bias[:, part] = jnp.sum(grad.astype(jnp.float32), axis=0, keepdims=True)
            grad_second[part, :] = lax.dot_general(
                hidden, frame_grad[...], (TN, ((), ())), preferred_element_type=jnp.float32
            )

    grad_first[...] = lax.dot_general(
        archive[...], d_pre[...], (TN, ((), ())), preferred_element_type=jnp.float32
    )


def finish(tau, total_pairs, parts, w_second, archive):
    frames, feat = parts[0].shape
    hid, field = w_second.shape[0], archive.shape[1]
    tile = 256

    def whole(shape):
        return pl.BlockSpec(shape, lambda i: (0,) * len(shape))

    return pl.pallas_call(
        functools.partial(finish_kernel, tau, total_pairs),
        grid=(field // tile,),
        out_shape=(
            jax.ShapeDtypeStruct((8, 128), jnp.float32),
            jax.ShapeDtypeStruct((field, hid), jnp.float32),
            jax.ShapeDtypeStruct((1, hid), jnp.float32),
            jax.ShapeDtypeStruct((hid, feat), jnp.float32),
        ),
        in_specs=[
            *(whole(part.shape) for part in parts),
            whole(w_second.shape),
            pl.BlockSpec((frames, tile), lambda i: (0, i)),
        ],
        out_specs=(
            whole((8, 128)),
            pl.BlockSpec((tile, hid), lambda i: (i, 0)),
            whole((1, hid)),
            whole((hid, feat)),
        ),
        scratch_shapes=[
            pltpu.VMEM((frames, feat), jnp.bfloat16),
            pltpu.VMEM((frames, hid), jnp.bfloat16),
            pltpu.VMEM((feat, feat), jnp.float32),
            pltpu.VMEM((feat, feat), jnp.float32),
        ],
        compiler_params=pltpu.CompilerParams(vmem_limit_bytes=52 * MIB),
        name="finish",
    )(*parts, w_second, archive)


def per_device(n, archive, w_first, b_first, w_second, pair_table):
    frames_total = archive.shape[0]
    steps_len = frames_total // TRAJS
    tau = frames_total // LAG_PARTS
    total_pairs = float(pair_table.shape[0] * n)
    columns = pair_table.T
    index = columns[2:3] * steps_len + columns[0:1]
    parts = exchange(n, tau, total_pairs, archive, w_first, b_first[None, :], w_second, index)
    score, grad_first, grad_bias, grad_second = finish(tau, total_pairs, parts, w_second, archive)
    return (score[0, :1], grad_first, grad_bias[0], grad_second)


def solution(mesh):
    placed = (
        P("group", "rep"),
        P(("group", "rep"), None),
        P("group"),
        P("group", None),
        P(("group", "rep"), None),
    )
    return jax.shard_map(
        functools.partial(per_device, mesh.shape["rep"]),
        mesh=mesh,
        in_specs=placed,
        out_specs=(P("group"), P(("group", "rep"), None), P("group"), P("group", None)),
        check_vma=False,
    )
```

```python
import functools

import jax
import jax.numpy as jnp
from jax import lax
from jax.experimental import pallas as pl
from jax.experimental.pallas import tpu as pltpu
from jax.sharding import PartitionSpec as P

TRAJS = 4
LAG_PARTS = 32
EPS = 0.001
MIB = 1 << 20


def elu(v):
    return jnp.where(v > 0, v, jnp.exp(jnp.minimum(v, 0.0)) - 1.0)


def exchange_kernel(
    n,
    tau,
    total_pairs,
    archive_hbm,
    w_first_hbm,
    b_hbm,
    w_second_hbm,
    index,
    feats,
    pre_all,
    weight,
    c00,
    ctt,
    c0t,
    inv0,
    invt,
    info,
    b_first,
    w_second,
    archive,
    w_first,
    load_sem,
    row_sem,
    column_sem,
    out_half,
    in_half,
    own_half,
    send_buf,
    recv_buf,
    index_all,
    pair_send,
    pair_recv,
    sum_send,
    sum_recv,
    cnt_send,
    cnt_recv,
    feat_send,
    feat_recv,
    pre_send,
    pre_recv,
):
    frames, hid = archive_hbm.shape[0], w_first_hbm.shape[1]
    half = frames // 2
    chips = n // 2
    rows = frames // n
    me = lax.axis_index("rep")
    core = lax.rem(me, 2)
    chip = me // 2
    partner = me + 1 - 2 * core

    def to(device):
        return {"rep": device}

    def peer_of(d):
        other = lax.rem(chip + d, chips)
        return other, other * 2 + core

    tile = 256
    piece = half // 2
    side_chips = chips // 2
    side = chip // side_chips

    def row_load(i):
        start = (1 - core if i % 2 == 0 else core) * half + (1 - side if i < 2 else side) * piece
        block = pl.ds(pl.multiple_of(start, 32), piece)
        return pltpu.make_async_copy(archive_hbm.at[block], archive.at[block], row_sem.at[i])

    def column_load(t):
        cols = pl.ds(pl.multiple_of(t * tile, tile), tile)
        return pltpu.make_async_copy(w_first_hbm.at[:, cols], w_first.at[:, cols], column_sem.at[t])

    row_load(0).start()
    for t in range(hid // tile):
        column_load(t).start()
    for i in range(1, 4):
        row_load(i).start()
    loads = [
        pltpu.make_async_copy(b_hbm, b_first, load_sem.at[0]),
        pltpu.make_async_copy(w_second_hbm, w_second, load_sem.at[1]),
    ]
    for load in loads:
        load.start()
    barrier = pltpu.get_barrier_semaphore()
    pl.semaphore_signal(barrier, inc=1, device_id=to(partner), device_id_type=pl.DeviceIdType.MESH)

    @pl.loop(1, chips)
    def _(d):
        pl.semaphore_signal(
            barrier, inc=1, device_id=to(peer_of(d)[1]), device_id_type=pl.DeviceIdType.MESH
        )

    def remote(src, dst, send, recv, device):
        return pltpu.make_async_remote_copy(
            src_ref=src,
            dst_ref=dst,
            send_sem=send,
            recv_sem=recv,
            device_id=to(device),
            device_id_type=pl.DeviceIdType.MESH,
        )

    def matmul(row0, nrows, dst, dst0, first=False):
        @pl.loop(0, hid // tile)
        def _(t):
            if first:
                column_load(t).wait()
            cols = pl.ds(pl.multiple_of(t * tile, tile), tile)
            dst[pl.ds(dst0, nrows), cols] = jnp.dot(
                archive[pl.ds(pl.multiple_of(row0, 32), nrows), :],
                w_first[:, cols],
                preferred_element_type=jnp.float32,
            )

    def sum_remote(other):
        return remote(
            send_buf.at[other],
            recv_buf.at[chip],
            sum_send.at[other],
            sum_recv.at[chip],
            other * 2 + core,
        )

    def send_sum(other):
        block = pl.ds(pl.multiple_of(other * rows, rows), rows)
        send_buf[other] = (own_half[block, :] + in_half[block, :]).astype(jnp.bfloat16)
        sum_remote(other).start()

    def partner_piece(which, index):
        start = pl.multiple_of(which * piece, 32)
        row_load(2 * index).wait()
        matmul((1 - core) * half + start, piece, out_half, start, index == 0)
        if index == 0:
            pl.semaphore_wait(barrier, chips)
        part = pl.ds(start, piece)
        copy = remote(
            out_half.at[part], in_half.at[part], pair_send.at[index], pair_recv.at[index], partner
        )
        copy.start()
        return copy

    def own_piece(which, index):
        start = pl.multiple_of(which * piece, 32)
        row_load(2 * index + 1).wait()
        matmul(core * half + start, piece, own_half, start)

    far_copy = partner_piece(1 - side, 0)
    own_piece(1 - side, 0)
    near_copy = partner_piece(side, 1)
    far_copy.wait_recv()

    @pl.loop(0, side_chips)
    def _(j):
        send_sum((1 - side) * side_chips + lax.rem(chip + j, side_chips))

    index_all[me] = jnp.broadcast_to(index[...], index_all.shape[1:])
    cnt_copy = remote(
        index_all.at[me], index_all.at[me], cnt_send.at[chips], cnt_recv.at[chips], partner
    )
    cnt_copy.start()
    own_piece(side, 1)
    near_copy.wait_recv()

    @pl.loop(1, side_chips)
    def _(j):
        send_sum(side * side_chips + lax.rem(chip + j, side_chips))

    cnt_copy.wait()
    for load in loads:
        load.wait()

    def cnt_remote(d):
        both = index_all.at[pl.ds(chip * 2, 2)]
        return remote(both, both, cnt_send.at[d], cnt_recv.at[chip], peer_of(d)[1])

    @pl.loop(1, chips)
    def _(d):
        cnt_remote(d).start()

    far_copy.wait_send()
    near_copy.wait_send()

    mine = pl.ds(pl.multiple_of(chip * rows, rows), rows)
    own_half[mine, :] = own_half[mine, :] + in_half[mine, :] + b_first[...]

    @pl.loop(1, chips)
    def _(d):
        other = peer_of(d)[0]
        remote(send_buf.at[other], recv_buf.at[other], sum_send.at[other], sum_recv.at[other], partner).wait_recv()
        own_half[mine, :] = own_half[mine, :] + recv_buf[other].astype(jnp.float32)

    pre_act = own_half[mine, :]
    hidden = elu(pre_act).astype(jnp.bfloat16)
    place = pl.ds(pl.multiple_of(core * half + chip * rows, rows), rows)
    feats[place, :] = jnp.dot(hidden, w_second[...], preferred_element_type=jnp.float32).astype(
        jnp.bfloat16
    )

    def gather_remote(buf, send, recv, d):
        return remote(buf.at[place], buf.at[place], send.at[d], recv.at[chip], peer_of(d)[1])

    @pl.loop(1, chips)
    def _(d):
        gather_remote(feats, feat_send, feat_recv, d).start()

    pre_all[place, :] = pre_act.astype(jnp.bfloat16)

    @pl.loop(1, chips)
    def _(d):
        gather_remote(pre_all, pre_send, pre_recv, d).start()

    def forward(buf, send, recv):
        @pl.loop(1, chips)
        def _(d):
            other = peer_of(d)[0]
            theirs = pl.ds(pl.multiple_of(core * half + other * rows, rows), rows)
            remote(buf.at[theirs], buf.at[theirs], send.at[d], recv.at[other], partner).wait_recv()

        side = pl.ds(pl.multiple_of(core * half, half), half)
        copy = remote(buf.at[side], buf.at[side], send.at[chips], recv.at[chips], partner)
        copy.start()
        return copy

    feat_copy = forward(feats, feat_send, feat_recv)

    @pl.loop(1, chips)
    def _(d):
        other = peer_of(d)[0]
        both = index_all.at[pl.ds(other * 2, 2)]
        remote(both, both, cnt_send.at[d], cnt_recv.at[other], partner).wait_recv()

    @pl.loop(0, frames // 128)
    def _(t):
        ids = t * 128 + lax.broadcasted_iota(jnp.int32, (128, index.shape[1]), 0)

        def add(r, total):
            return total + (index_all[r][0:1, :] == ids).astype(jnp.float32)

        total = lax.fori_loop(0, n, add, jnp.zeros(ids.shape, jnp.float32))
        weight[pl.ds(pl.multiple_of(t * 128, 128), 128), :] = jnp.sum(
            total, axis=1, keepdims=True
        )

    feat_copy.wait()
    start_inverse(tau, total_pairs, feats, weight, c00, ctt, c0t, inv0, invt, info)
    refine(6, c00, ctt, inv0, invt, info)
    pre_copy = forward(pre_all, pre_send, pre_recv)
    refine(3, c00, ctt, inv0, invt, info)
    pre_copy.wait()

    @pl.loop(1, chips)
    def _(d):
        cnt_remote(d).wait_send()
        sum_remote(peer_of(d)[0]).wait_send()
        gather_remote(feats, feat_send, feat_recv, d).wait_send()
        gather_remote(pre_all, pre_send, pre_recv, d).wait_send()


def exchange(n, tau, total_pairs, archive, w_first, b_first, w_second, index):
    frames, hid, feat = archive.shape[0], w_first.shape[1], w_second.shape[1]
    half, chips, rows = frames // 2, n // 2, frames // n
    vmem = pl.BlockSpec(memory_space=pltpu.VMEM)
    hbm = pl.BlockSpec(memory_space=pltpu.HBM)
    dma = pltpu.SemaphoreType.DMA
    square = jax.ShapeDtypeStruct((feat, feat), jnp.float32)
    return pl.pallas_call(
        functools.partial(exchange_kernel, n, tau, total_pairs),
        out_shape=(
            jax.ShapeDtypeStruct((frames, feat), jnp.bfloat16),
            jax.ShapeDtypeStruct((frames, hid), jnp.bfloat16),
            jax.ShapeDtypeStruct((frames, 1), jnp.float32),
            square,
            square,
            square,
            square,
            square,
            jax.ShapeDtypeStruct((8, 128), jnp.float32),
        ),
        in_specs=[hbm, hbm, hbm, hbm, vmem],
        out_specs=(vmem,) * 9,
        scratch_shapes=[
            pltpu.VMEM(b_first.shape, jnp.float32),
            pltpu.VMEM(w_second.shape, jnp.bfloat16),
            pltpu.VMEM(archive.shape, jnp.bfloat16),
            pltpu.VMEM(w_first.shape, jnp.bfloat16),
            dma((2,)),
            dma((4,)),
            dma((hid // 256,)),
            pltpu.VMEM((half, hid), jnp.float32),
            pltpu.VMEM((half, hid), jnp.float32),
            pltpu.VMEM((half, hid), jnp.float32),
            pltpu.VMEM((chips, rows, hid), jnp.bfloat16),
            pltpu.VMEM((chips, rows, hid), jnp.bfloat16),
            pltpu.VMEM((n, 8, index.shape[1]), jnp.int32),
            dma((2,)),
            dma((2,)),
            dma((chips,)),
            dma((chips,)),
            dma((chips + 1,)),
            dma((chips + 1,)),
            dma((chips + 1,)),
            dma((chips + 1,)),
            dma((chips + 1,)),
            dma((chips + 1,)),
        ],
        compiler_params=pltpu.CompilerParams(
            collective_id=0, has_side_effects=True, vmem_limit_bytes=52 * MIB
        ),
        name="exchange",
    )(archive, w_first, b_first, w_second, index)


def mm(a, b, dims=((1,), (0,))):
    a_top, b_top = a.astype(jnp.bfloat16), b.astype(jnp.bfloat16)
    a_rest = (a - a_top.astype(jnp.float32)).astype(jnp.bfloat16)
    b_rest = (b - b_top.astype(jnp.float32)).astype(jnp.bfloat16)

    def dot(x, y):
        return lax.dot_general(x, y, (dims, ((), ())), preferred_element_type=jnp.float32)

    return dot(a_top, b_top) + (dot(a_top, b_rest) + dot(a_rest, b_top))


TN = ((0,), (0,))
NT = ((1,), (1,))


def identity(feat):
    return (
        lax.broadcasted_iota(jnp.int32, (feat, feat), 0)
        == lax.broadcasted_iota(jnp.int32, (feat, feat), 1)
    ).astype(jnp.float32)


def centred_rows(tau, scale, feats, n):
    first = feats[...].astype(jnp.float32)
    later = jnp.concatenate([first[tau:], first[:tau]], axis=0)
    x0 = first - jnp.sum(first * n, axis=0, keepdims=True) * scale
    xt = later - jnp.sum(later * n, axis=0, keepdims=True) * scale
    return x0, xt


def gain(low):
    return 4.0 / ((1.0 + low) * (1.0 + low))


def start_inverse(tau, total_pairs, feats, weight, c00, ctt, c0t, inv0, invt, info):
    n = weight[...]
    scale = 1.0 / total_pairs
    x0, xt = centred_rows(tau, scale, feats, n)
    x0n = x0 * (n * scale)
    eye = identity(feats.shape[1])
    first = mm(x0n, x0, TN) + EPS * eye
    c0t[...] = mm(x0n, xt, TN)
    later = mm(xt * (n * scale), xt, TN) + EPS * eye
    top0 = jnp.max(jnp.sum(jnp.abs(first), axis=0, keepdims=True), axis=1, keepdims=True)
    topt = jnp.max(jnp.sum(jnp.abs(later), axis=0, keepdims=True), axis=1, keepdims=True)
    first = first / top0
    later = later / topt
    low = EPS / jnp.maximum(top0, topt)
    c00[...] = first
    ctt[...] = later
    inv0[...] = gain(low) * ((1.0 + low) * eye - first)
    invt[...] = gain(low) * ((1.0 + low) * eye - later)
    info[0:1, :] = jnp.broadcast_to(top0, (1, 128))
    info[1:2, :] = jnp.broadcast_to(topt, (1, 128))
    info[2:3, :] = jnp.broadcast_to(jnp.minimum(gain(low) * low, 1.0), (1, 128))


def newton_step(c00, ctt, inv0, invt, low):
    eye = identity(c00.shape[0])
    a, b = inv0[...], invt[...]
    ra = (1.0 + low) * eye - mm(c00[...], a)
    rb = (1.0 + low) * eye - mm(ctt[...], b)
    inv0[...] = gain(low) * mm(a, ra)
    invt[...] = gain(low) * mm(b, rb)
    return jnp.minimum(gain(low) * low, 1.0)


def refine(steps, c00, ctt, inv0, invt, info):
    @pl.loop(0, steps)
    def _(_):
        low = newton_step(c00, ctt, inv0, invt, info[2:3, 0:1])
        info[2:3, :] = jnp.broadcast_to(low, (1, 128))


def score_into(
    tau, total_pairs, feats, weight, c00, ctt, c0t, start0, startt, info, score, frame_grad, inv0, invt
):
    inv0[...] = start0[...]
    invt[...] = startt[...]
    lax.while_loop(
        lambda low: jnp.max(low) < 1.0 - 2e-6,
        lambda low: newton_step(c00, ctt, inv0, invt, low),
        info[2:3, 0:1],
    )
    a = inv0[...] / info[0:1, 0:1]
    b = invt[...] / info[1:2, 0:1]
    cross = c0t[...]
    u = mm(a, cross)
    v = mm(cross, b)
    k = mm(u, b)
    score[...] = jnp.broadcast_to(1.0 + jnp.sum(u * v), score.shape)
    g00 = -2.0 * mm(k, u, NT)
    gtt = -2.0 * mm(k, v, TN)
    k = 2.0 * k
    n = weight[...]
    scale = 1.0 / total_pairs
    x0, xt = centred_rows(tau, scale, feats, n)
    n = n * scale
    frames = feats.shape[0]
    d0 = n * (mm(x0, g00) + mm(xt, k, NT))
    dt = n * (mm(x0, k) + mm(xt, gtt))
    dt = jnp.concatenate([dt[frames - tau :], dt[: frames - tau]], axis=0)
    frame_grad[...] = (d0 + dt).astype(jnp.bfloat16)


def finish_kernel(
    tau,
    total_pairs,
    feats,
    pre_act,
    weight,
    c00,
    ctt,
    c0t,
    start0,
    startt,
    info,
    w_second,
    archive,
    score,
    grad_first,
    grad_bias,
    grad_second,
    frame_grad,
    d_pre,
    inv0,
    invt,
):
    tile = feats.shape[1]

    @pl.when(pl.program_id(0) == 0)
    def _():
        score_into(
            tau,
            total_pairs,
            feats,
            weight,
            c00,
            ctt,
            c0t,
            start0,
            startt,
            info,
            score,
            frame_grad,
            inv0,
            invt,
        )

        @pl.loop(0, d_pre.shape[1] // tile)
        def _(t):
            part = pl.ds(pl.multiple_of(t * tile, tile), tile)
            pre = pre_act[:, part].astype(jnp.float32)
            low_exp = jnp.exp(jnp.minimum(pre, 0.0))
            positive = pre > 0
            hidden = jnp.where(positive, pre, low_exp - 1.0).astype(jnp.bfloat16)
            back = lax.dot_general(
                frame_grad[...],
                w_second[part, :],
                (NT, ((), ())),
                preferred_element_type=jnp.float32,
            )
            grad = (back * jnp.where(positive, 1.0, low_exp)).astype(jnp.bfloat16)
            d_pre[:, part] = grad
            grad_bias[:, part] = jnp.sum(grad.astype(jnp.float32), axis=0, keepdims=True)
            grad_second[part, :] = lax.dot_general(
                hidden, frame_grad[...], (TN, ((), ())), preferred_element_type=jnp.float32
            )

    grad_first[...] = lax.dot_general(
        archive[...], d_pre[...], (TN, ((), ())), preferred_element_type=jnp.float32
    )


def finish(tau, total_pairs, parts, w_second, archive):
    frames, feat = parts[0].shape
    hid, field = w_second.shape[0], archive.shape[1]
    tile = 256

    def whole(shape):
        return pl.BlockSpec(shape, lambda i: (0,) * len(shape))

    return pl.pallas_call(
        functools.partial(finish_kernel, tau, total_pairs),
        grid=(field // tile,),
        out_shape=(
            jax.ShapeDtypeStruct((8, 128), jnp.float32),
            jax.ShapeDtypeStruct((field, hid), jnp.float32),
            jax.ShapeDtypeStruct((1, hid), jnp.float32),
            jax.ShapeDtypeStruct((hid, feat), jnp.float32),
        ),
        in_specs=[
            *(whole(part.shape) for part in parts),
            whole(w_second.shape),
            pl.BlockSpec((frames, tile), lambda i: (0, i)),
        ],
        out_specs=(
            whole((8, 128)),
            pl.BlockSpec((tile, hid), lambda i: (i, 0)),
            whole((1, hid)),
            whole((hid, feat)),
        ),
        scratch_shapes=[
            pltpu.VMEM((frames, feat), jnp.bfloat16),
            pltpu.VMEM((frames, hid), jnp.bfloat16),
            pltpu.VMEM((feat, feat), jnp.float32),
            pltpu.VMEM((feat, feat), jnp.float32),
        ],
        compiler_params=pltpu.CompilerParams(vmem_limit_bytes=52 * MIB),
        name="finish",
    )(*parts, w_second, archive)


def per_device(n, archive, w_first, b_first, w_second, pair_table):
    frames_total = archive.shape[0]
    steps_len = frames_total // TRAJS
    tau = frames_total // LAG_PARTS
    total_pairs = float(pair_table.shape[0] * n)
    columns = pair_table.T
    index = columns[2:3] * steps_len + columns[0:1]
    parts = exchange(n, tau, total_pairs, archive, w_first, b_first[None, :], w_second, index)
    score, grad_first, grad_bias, grad_second = finish(tau, total_pairs, parts, w_second, archive)
    return (score[0, :1], grad_first, grad_bias[0], grad_second)


def solution(mesh):
    placed = (
        P("group", "rep"),
        P(("group", "rep"), None),
        P("group"),
        P("group", None),
        P(("group", "rep"), None),
    )
    return jax.shard_map(
        functools.partial(per_device, mesh.shape["rep"]),
        mesh=mesh,
        in_specs=placed,
        out_specs=(P("group"), P(("group", "rep"), None), P("group"), P("group", None)),
        check_vma=False,
    )
```
